32 devices in a mesh: dp: 16 (over z, x, core), tensor: 2 (over y).
Axes of the slice: x: 2, y: 2, z: 4, core: 2. Of those that a mesh axis runs over, the one named last changes fastest.
Arguments:
- tokens: bfloat16 [16384, 1024], P('dp'), may hold values from -6 to 6
- out_grad: bfloat16 [16384, 1024], P('dp'), may hold values from -6 to 6
- segment_ids: int32 [16384], P('dp'), may hold values from -1 to 31, as said below
- norm_gains: float32 [2, 1024], replicated, may hold values from 0.25 to 1.75
- w_zx: bfloat16 [1024, 2, 1536], P(None, None, 'tensor'), may hold values from -0.1875 to 0.1875
- w_bc: bfloat16 [1024, 256], replicated, may hold values from -0.1875 to 0.1875
- w_dt: bfloat16 [1024, 24], P(None, 'tensor'), may hold values from -0.1875 to 0.1875
- conv_x: float32 [5, 1536], P(None, 'tensor'), may hold values from -3 to 3
- conv_bc: float32 [5, 256], replicated, may hold values from -3 to 3
- head_params: float32 [3, 24], P(None, 'tensor'), may hold values from -4 to 1.5
- ssm_gain: float32 [1536], P('tensor'), may hold values from 0.25 to 1.75
- w_out: bfloat16 [1536, 1024], P('tensor'), may hold values from -0.15625 to 0.15625
- w_q: bfloat16 [1024, 512], P(None, 'tensor'), may hold values from -0.1875 to 0.1875
- w_kv: bfloat16 [1024, 2, 128], P(None, None, 'tensor'), may hold values from -0.1875 to 0.1875
- w_o: bfloat16 [512, 1024], P('tensor'), may hold values from -6 to 6
- w_gate_up: bfloat16 [1024, 2, 2048], P(None, None, 'tensor'), may hold values from -0.1875 to 0.1875
- w_down: bfloat16 [2048, 1024], P('tensor'), may hold values from -0.125 to 0.125
Outputs:
- mixed: bfloat16 [16384, 1024], P('dp')
- grad_tokens: float32 [16384, 1024], P('dp')
- grad_norm_gains: float32 [2, 1024], P(None, ('dp', 'tensor'))
- grad_w_zx: float32 [1024, 2, 1536], P('dp', None, 'tensor')
- grad_w_bc: float32 [1024, 256], P(('dp', 'tensor'))
- grad_w_dt: float32 [1024, 24], P('dp', 'tensor')
- grad_conv_x: float32 [5, 1536], P(None, 'tensor')
- grad_conv_bc: float32 [5, 256], P(None, ('dp', 'tensor'))
- grad_head_params: float32 [3, 24], P(None, 'tensor')
- grad_ssm_gain: float32 [1536], P('tensor')
- grad_w_out: float32 [1536, 1024], P('tensor', 'dp')
- grad_w_q: float32 [1024, 512], P('dp', 'tensor')
- grad_w_kv: float32 [1024, 2, 128], P('dp', None, 'tensor')
- grad_w_o: float32 [512, 1024], P('tensor', 'dp')
- grad_w_gate_up: float32 [1024, 2, 2048], P('dp', None, 'tensor')
- grad_w_down: float32 [2048, 1024], P('tensor', 'dp')
The draws below stay inside these ranges and needn't reach their ends.
Inputs may be any that keep to these rules, and one draw needn't show every extreme that they name: `segment_ids`: equal numbers form contiguous runs inside one block of 1024 slots and rise along the slots; -1 marks empty slots at a block's end; each sequence has 512 to 1024 tokens, each block holds one or two sequences, and some block is full.
All inputs are finite; a program needn't handle non-finite values.
Results may differ from the reference program's by a relative error of at most 0.012.
Values sent between devices are 32-bit elements; how exact they have to be, the bound alone decides.
A program may use at most 256 MiB of HBM per device.

```python
import math
import jax
import jax.numpy as jnp
from jax import lax

D = 1024
FF = 2048
SSM_HEADS = 24
SSM_HEAD_DIM = 64
STATE = 128
CONV = 4
Q_HEADS = 8
KV_HEADS = 2
ATT_HEAD_DIM = 64
SPAN = 128
SEQ_MIN = 512
INNER = 1536
TOK_DEV = 1024
TOKENS = 16384


def draw_segment_ids(key, part):
    key = jax.random.fold_in(key, 11)
    first_key, second_key = jax.random.split(key)
    blocks = TOKENS // TOK_DEV
    lengths = jax.random.randint(first_key, (blocks,), SEQ_MIN, 2 * SEQ_MIN + 1, dtype=jnp.int32)
    paired = jax.random.randint(second_key, (blocks,), 0, 4, dtype=jnp.int32) == 0
    lengths = lengths.at[1].set(2 * SEQ_MIN).at[2].set(SEQ_MIN)
    paired = paired.at[0].set(True).at[1].set(False).at[2].set(False).at[blocks - 1].set(True)
    lengths = jnp.where(paired, SEQ_MIN, lengths)
    slots = jnp.arange(TOK_DEV, dtype=jnp.int32)[None, :]
    local = jnp.where(slots < lengths[:, None], 0, jnp.where(paired[:, None], 1, -1))
    block_index = jnp.arange(blocks, dtype=jnp.int32)[:, None]
    numbers = jnp.where(local >= 0, 2 * block_index + local, -1)
    return numbers.reshape(TOKENS).astype(jnp.int32)


def draw_head_params(key, part):
    key = jax.random.fold_in(key, 23)
    keys = jax.random.split(key, 3)
    log_rates = jax.random.uniform(keys[0], (SSM_HEADS,), jnp.float32, -4.0, 1.0)
    offsets = jax.random.uniform(keys[1], (SSM_HEADS,), jnp.float32, -3.0, 0.0)
    skips = jax.random.uniform(keys[2], (SSM_HEADS,), jnp.float32, 0.5, 1.5)
    return jnp.stack([log_rates, offsets, skips])


def spiked(values, key, source, target, shards_of, factor):
    def block_of(dim):
        return (jnp.arange(values.shape[dim]) // (values.shape[dim] // shards_of)).reshape((-1,) + (1,) * (values.ndim - 1 - dim))

    near = jax.random.permutation(key, shards_of)[block_of(target)]
    other_side = (block_of(target) + shards_of // 2) % shards_of
    return jnp.where((block_of(source) == near) | (block_of(source) == other_side), factor * values, values)


def block_scale(own_key, shape, shards, least, high):
    factor_of = 1.0
    for dim, shards_of in shards:
        draws = jax.random.uniform(jax.random.fold_in(jax.random.fold_in(own_key, 6), dim), (shards_of,), jnp.float32, least / len(shards), high / len(shards))
        factor_of = factor_of * jnp.repeat(jnp.exp(draws), shape[dim] // shards_of).reshape((-1,) + (1,) * (len(shape) - 1 - dim))
    return factor_of


def gaussian(key, shape, spread, reach, shards=(), kind=jnp.bfloat16):
    drawn = jax.random.normal(key, shape, jnp.float32) * spread
    if len(shards) > 0:
        drawn = block_scale(key, shape, shards, -0.22, 0.18) * drawn
    return jnp.clip(drawn, min=-reach, max=reach).astype(kind)


def bell_draw_with(key, shape, deviation, reach, pieces, heavy, kind=jnp.bfloat16):
    values = deviation * jax.random.normal(key, shape, jnp.float32)
    if pieces:
        values = values * block_scale(key, shape, pieces, -0.22, 0.18)
    return jnp.clip(spiked(values, jax.random.fold_in(key, 3), *heavy), -reach, reach).astype(kind)


def setup_inputs(seed: int = 0) -> dict:
    arg_keys = jax.random.split(jax.random.key(seed), 18)
    return {
        "tokens": gaussian(arg_keys[0], (TOKENS, D), 1.0, 6.0, ((0, 16),)),
        "out_grad": bell_draw_with(arg_keys[1], (TOKENS, D), 1.0, 6.0, ((0, 16),), (0, 1, 16, 2.0)),
        "segment_ids": draw_segment_ids(jax.random.fold_in(arg_keys[17], 71), 0),
        "norm_gains": jnp.clip(1.0 + 0.15 * jax.random.normal(arg_keys[3], (2, D), jnp.float32), 0.25, 1.75),
        "w_zx": gaussian(arg_keys[4], (D, 2, INNER), D ** -0.5, 0.1875, ((2, 2),)),
        "w_bc": gaussian(arg_keys[5], (D, 2 * STATE), D ** -0.5, 0.1875),
        "w_dt": gaussian(arg_keys[6], (D, SSM_HEADS), D ** -0.5, 0.1875, ((1, 2),)),
        "conv_x": gaussian(arg_keys[7], (CONV + 1, INNER), 0.5, 3.0, ((1, 2),), jnp.float32),
        "conv_bc": gaussian(arg_keys[8], (CONV + 1, 2 * STATE), 0.5, 3.0, (), jnp.float32),
        "head_params": draw_head_params(jax.random.fold_in(arg_keys[17], 71), 0),
        "ssm_gain": jnp.clip(1.0 + 0.15 * jax.random.normal(arg_keys[10], (INNER,), jnp.float32), 0.25, 1.75),
        "w_out": gaussian(arg_keys[11], (INNER, D), INNER ** -0.5, 0.15625, ((0, 2),)),
        "w_q": gaussian(arg_keys[12], (D, Q_HEADS * ATT_HEAD_DIM), D ** -0.5, 0.1875, ((1, 2),)),
        "w_kv": gaussian(arg_keys[13], (D, 2, KV_HEADS * ATT_HEAD_DIM), D ** -0.5, 0.1875, ((2, 2),)),
        "w_o": gaussian(arg_keys[14], (Q_HEADS * ATT_HEAD_DIM, D), (max(1, Q_HEADS * ATT_HEAD_DIM // (2 * SEQ_MIN))) ** -0.5, 6.0, ((0, 2),)),
        "w_gate_up": gaussian(arg_keys[15], (D, 2, FF), D ** -0.5, 0.1875, ((2, 2),)),
        "w_down": gaussian(arg_keys[16], (FF, D), FF ** -0.5, 0.125, ((0, 2),)),
    }


EPS = 1e-05
ROPE_BASE = 100000000000.0

@jax.custom_vjp
def low(v):
    return lax.optimization_barrier(v.astype(jnp.bfloat16)).astype(jnp.float32)

@jax.custom_vjp
def low_back(v):
    return v

def low_keep(v):
    return (low(v), None)

def low_pass(kept, grad):
    return (grad,)

def back_keep(v):
    return (v, None)

def back_low(kept, grad):
    return (low(grad),)
low.defvjp(low_keep, low_pass)
low_back.defvjp(back_keep, back_low)

def matmul(left, right):
    return jnp.dot(left, right, preferred_element_type=jnp.float32, precision=lax.Precision.HIGHEST)

def norm_scale(values):
    return lax.rsqrt(lax.optimization_barrier(jnp.mean(values * values, axis=-1, keepdims=True)) + EPS)

def token_places(segments):
    count = segments.shape[0]
    index = jnp.arange(count, dtype=jnp.int32)
    starts = jnp.concatenate([jnp.ones((1,), dtype=bool), segments[1:] != segments[:-1]])
    first = lax.cummax(jnp.where(starts, index, 0), axis=0)
    return (index - first).astype(jnp.float32)

def rotary_tables(places, head_dim):
    half = head_dim // 2
    freqs = jnp.exp(jnp.arange(half, dtype=jnp.float32) * (-2.0 * math.log(ROPE_BASE) / head_dim))
    angle = places[:, None] * freqs[None, :]
    return (jnp.cos(angle), jnp.sin(angle))

def rotate(values, cosines, sines):
    half = values.shape[-1] // 2
    first = values[..., :half]
    second = values[..., half:]
    cosines = cosines[:, None, :]
    sines = sines[:, None, :]
    return jnp.concatenate([first * cosines - second * sines, second * cosines + first * sines], axis=-1)

def causal_filter(values, taps, segments):
    total = values.shape[0]
    width = taps.shape[0] - 1
    result = taps[width][None, :] + taps[0][None, :] * values
    for offset in range(1, width):
        earlier = jnp.concatenate([jnp.zeros((offset, values.shape[1]), values.dtype), values[:total - offset]])
        earlier_seg = jnp.concatenate([jnp.full((offset,), -2, jnp.int32), segments[:total - offset]])
        result = result + jnp.where((earlier_seg == segments)[:, None], earlier, 0.0) * taps[offset][None, :]
    return result

def state_space(inputs, steps, rates, b_mat, c_mat, segments):
    total, heads, head_dim = inputs.shape
    nstate = b_mat.shape[1]
    count = total // SPAN
    x_blocks = inputs.reshape(count, SPAN, heads, head_dim)
    step_blocks = steps.reshape(count, SPAN, heads)
    b_blocks = b_mat.reshape(count, SPAN, nstate)
    c_blocks = c_mat.reshape(count, SPAN, nstate)
    seg_blocks = segments.reshape(count, SPAN)
    decay_sum = jnp.cumsum(-step_blocks * rates[None, None, :], axis=1)
    inside = (seg_blocks[:, :, None] == seg_blocks[:, None, :]) & jnp.tril(jnp.ones((SPAN, SPAN), dtype=bool))[None]
    inside = inside[..., None]
    gap = decay_sum[:, :, None, :] - decay_sum[:, None, :, :]
    weights = jnp.exp(jnp.where(inside, gap, 0.0)) * inside.astype(jnp.float32)
    intersection = jnp.einsum('cin,cjn->cij', c_blocks, b_blocks, precision=lax.Precision.HIGHEST)
    weights = weights * intersection[..., None] * step_blocks[:, None, :, :]
    within = jnp.einsum('cijh,cjhp->cihp', weights, x_blocks, precision=lax.Precision.HIGHEST)
    last_seg = seg_blocks[:, -1]
    final = decay_sum[:, -1, :]
    tail = (seg_blocks == last_seg[:, None]).astype(jnp.float32)[:, :, None] * jnp.exp(final[:, None, :] - decay_sum) * step_blocks
    block_state = jnp.einsum('cjh,cjhp,cjn->chpn', tail, x_blocks, b_blocks, precision=lax.Precision.HIGHEST)
    carry_on = jnp.concatenate([jnp.zeros((1,), jnp.float32), (last_seg[1:] == last_seg[:-1]).astype(jnp.float32)])
    factor = jnp.exp(final) * carry_on[:, None]

    def advance(state, pair):
        new_state = pair[0][:, None, None] * state + pair[1]
        return (new_state, state)
    unused, entering = lax.scan(advance, jnp.zeros((heads, head_dim, nstate), jnp.float32), (factor, block_state))
    previous = jnp.concatenate([jnp.full((1,), -3, jnp.int32), last_seg[:-1]])
    head_weight = (seg_blocks == previous[:, None]).astype(jnp.float32)[:, :, None] * jnp.exp(decay_sum)
    carried = jnp.einsum('cin,chpn->cihp', c_blocks, entering, precision=lax.Precision.HIGHEST) * head_weight[..., None]
    return (within + carried).reshape(total, heads, head_dim)

def mixer_core(gate_and_x, step_raw, state_maps, conv_x, conv_bc, head_params, segments):
    total = gate_and_x.shape[0]
    heads = step_raw.shape[1]
    z_part = gate_and_x[:, 0]
    x_part = jax.nn.silu(causal_filter(gate_and_x[:, 1], conv_x, segments))
    maps = jax.nn.silu(causal_filter(state_maps, conv_bc, segments))
    nstate = state_maps.shape[1] // 2
    x_heads = x_part.reshape(total, heads, SSM_HEAD_DIM)
    rates = jnp.exp(head_params[0])
    steps = jax.nn.softplus(step_raw + head_params[1][None, :])
    output = state_space(x_heads, steps, rates, maps[:, :nstate], maps[:, nstate:], segments)
    output = output + head_params[2][None, :, None] * x_heads
    return output.reshape(total, heads * SSM_HEAD_DIM) * jax.nn.silu(z_part)

def attention_ref(queries, keys, values, segments):
    total = queries.shape[0]
    block = min(512, total)
    scale = queries.shape[-1] ** (-0.5)
    index = jnp.arange(total, dtype=jnp.int32)

    def one_block(start):
        part = lax.dynamic_slice_in_dim(queries, start, block, 0)
        part_seg = lax.dynamic_slice_in_dim(segments, start, block, 0)
        scores = low_back(jnp.einsum('ikgd,jkd->kgij', part, keys, precision=lax.Precision.HIGHEST) * scale)
        rows_here = start + jnp.arange(block, dtype=jnp.int32)
        allowed = (part_seg[:, None] == segments[None, :]) & (rows_here[:, None] >= index[None, :])
        scores = jnp.where(allowed[None, None], scores, -1e+30)
        probs = jnp.exp(scores - jax.nn.logsumexp(scores, axis=-1, keepdims=True))
        return jnp.einsum('kgij,jkd->ikgd', low(probs), values, precision=lax.Precision.HIGHEST)
    starts = jnp.arange(total // block, dtype=jnp.int32) * block
    result = lax.map(jax.checkpoint(one_block), starts)
    return result.reshape(queries.shape)

def block_forward(resid, segments, params):
    gains, w_zx, w_bc, w_dt, conv_x, conv_bc, head_params, ssm_gain, w_out, w_q, w_kv, w_o, w_gate_up, w_down = params
    total = resid.shape[0]
    group = Q_HEADS // KV_HEADS
    normed_in = low(resid * norm_scale(resid) * gains[0])
    gate_and_x = low_back(matmul(normed_in, w_zx.reshape(D, 2 * INNER))).reshape(total, 2, INNER)
    step_raw = low_back(matmul(normed_in, w_dt))
    state_maps = matmul(normed_in, w_bc)
    gated = mixer_core(gate_and_x, step_raw, state_maps, conv_x, conv_bc, head_params, segments)
    mixed_ssm = low(gated * norm_scale(gated) * ssm_gain)
    cosines, sines = rotary_tables(token_places(segments), ATT_HEAD_DIM)
    queries = low_back(matmul(normed_in, w_q)).reshape(total, Q_HEADS, ATT_HEAD_DIM)
    key_vals = low_back(matmul(normed_in, w_kv.reshape(D, 2 * KV_HEADS * ATT_HEAD_DIM))).reshape(total, 2, KV_HEADS, ATT_HEAD_DIM)
    queries = low(rotate(queries, cosines, sines)).reshape(total, KV_HEADS, group, ATT_HEAD_DIM)
    keys = low(rotate(key_vals[:, 0], cosines, sines))
    values = low(key_vals[:, 1])
    attended = low(low_back(attention_ref(queries, keys, values, segments))).reshape(total, Q_HEADS * ATT_HEAD_DIM)
    mixer = low_back(matmul(mixed_ssm, w_out) + matmul(attended, w_o))
    middle = resid + mixer
    normed_mid = low(middle * norm_scale(middle) * gains[1])
    gate_up = low_back(matmul(normed_mid, w_gate_up.reshape(D, 2 * FF))).reshape(total, 2, FF)
    activation = low(jax.nn.silu(gate_up[:, 0]) * gate_up[:, 1])
    return middle + low_back(matmul(activation, w_down))

def reference(tokens, out_grad, segment_ids, norm_gains, w_zx, w_bc, w_dt, conv_x, conv_bc, head_params, ssm_gain, w_out, w_q, w_kv, w_o, w_gate_up, w_down):
    blocks = TOKENS // TOK_DEV
    resid = tokens.astype(jnp.float32).reshape(blocks, TOK_DEV, D)
    segments = segment_ids.astype(jnp.int32).reshape(blocks, TOK_DEV)
    live = (segments >= 0).astype(jnp.float32)[..., None]
    cotangent = out_grad.astype(jnp.float32).reshape(blocks, TOK_DEV, D) * live
    params = (norm_gains.astype(jnp.float32), w_zx.astype(jnp.float32), w_bc.astype(jnp.float32), w_dt.astype(jnp.float32), conv_x.astype(jnp.float32), conv_bc.astype(jnp.float32), head_params.astype(jnp.float32), ssm_gain.astype(jnp.float32), w_out.astype(jnp.float32), w_q.astype(jnp.float32), w_kv.astype(jnp.float32), w_o.astype(jnp.float32), w_gate_up.astype(jnp.float32), w_down.astype(jnp.float32))

    def whole(resid_all, param_all):

        def one(pair):
            return jax.checkpoint(block_forward)(pair[0], pair[1], param_all)
        return lax.map(one, (resid_all, segments))
    result, pullback = jax.vjp(whole, resid, params)
    grad_resid, grads = pullback(cotangent)
    return (result.reshape(TOKENS, D).astype(jnp.bfloat16), grad_resid.reshape(TOKENS, D), grads[0], grads[1], grads[2], grads[3], grads[4], grads[5], grads[6], grads[7], grads[8], grads[9], grads[10], grads[11], grads[12], grads[13])
```

```python
import math

import jax
import jax.numpy as jnp
from jax import lax
from jax.sharding import PartitionSpec as P

SSM_HEAD_DIM = 64
ATT_HEAD_DIM = 64
SPAN = 128
INNER = 1536
ATT_BLOCK = 256
PIECES = 2
PRECISE = lax.Precision.HIGH


EPS = 1e-05
ROPE_BASE = 100000000000.0


def product(left, right):
    return jnp.dot(left, right, preferred_element_type=jnp.float32)


def product_back(left, right):
    return lax.dot_general(
        left, right, (((1,), (1,)), ((), ())), preferred_element_type=jnp.float32
    )


def weight_product(left, right):
    return lax.dot_general(
        left, right, (((0,), (0,)), ((), ())), preferred_element_type=jnp.float32
    )


def norm_scale(values):
    return lax.rsqrt(jnp.mean(values * values, axis=-1, keepdims=True) + EPS)


def norm_back(grad_normed, unit, scale, gain):
    grad_unit = grad_normed * gain[None, :]
    return scale * (grad_unit - unit * jnp.mean(grad_unit * unit, axis=-1, keepdims=True))


def token_places(segments):
    count = segments.shape[0]
    index = jnp.arange(count, dtype=jnp.int32)
    starts = jnp.concatenate([jnp.ones((1,), dtype=bool), segments[1:] != segments[:-1]])
    first = lax.cummax(jnp.where(starts, index, 0), axis=0)
    return (index - first).astype(jnp.float32)


def rotary_tables(places, head_dim):
    half = head_dim // 2
    freqs = jnp.exp(jnp.arange(half, dtype=jnp.float32) * (-2.0 * math.log(ROPE_BASE) / head_dim))
    angle = places[:, None] * freqs[None, :]
    return (jnp.cos(angle), jnp.sin(angle))


def rotate(values, cosines, sines):
    half = values.shape[-1] // 2
    first = values[..., :half]
    second = values[..., half:]
    cosines = cosines[:, None, :]
    sines = sines[:, None, :]
    return jnp.concatenate(
        [first * cosines - second * sines, second * cosines + first * sines], axis=-1
    )


def rotate_back(grads, cosines, sines):
    half = grads.shape[-1] // 2
    first = grads[..., :half]
    second = grads[..., half:]
    cosines = cosines[:, None, :]
    sines = sines[:, None, :]
    return jnp.concatenate(
        [first * cosines + second * sines, second * cosines - first * sines], axis=-1
    )


def causal_filter(values, taps, segments):
    total = values.shape[0]
    width = taps.shape[0] - 1
    result = taps[width][None, :] + taps[0][None, :] * values
    for offset in range(1, width):
        earlier = jnp.concatenate(
            [jnp.zeros((offset, values.shape[1]), values.dtype), values[: total - offset]]
        )
        earlier_seg = jnp.concatenate(
            [jnp.full((offset,), -2, jnp.int32), segments[: total - offset]]
        )
        result = (
            result
            + jnp.where((earlier_seg == segments)[:, None], earlier, 0.0) * taps[offset][None, :]
        )
    return result


def state_space(inputs, steps, rates, b_mat, c_mat, segments):
    total, heads, head_dim = inputs.shape
    nstate = b_mat.shape[1]
    count = total // SPAN
    step_blocks = steps.reshape(count, SPAN, heads).transpose(0, 2, 1)
    x_blocks = inputs.reshape(count, SPAN, heads, head_dim).transpose(0, 2, 1, 3)
    x_blocks = x_blocks * step_blocks[..., None]
    b_blocks = b_mat.reshape(count, SPAN, nstate)
    c_blocks = c_mat.reshape(count, SPAN, nstate)
    seg_blocks = segments.reshape(count, SPAN)
    lower = jnp.tril(jnp.ones((SPAN, SPAN), jnp.float32))
    decay_sum = jnp.einsum(
        "chj,ij->chi", -step_blocks * rates[None, :, None], lower, precision=lax.Precision.HIGHEST
    )
    inside = (seg_blocks[:, :, None] == seg_blocks[:, None, :]) & (lower > 0)[None]
    gap = decay_sum[:, :, :, None] - decay_sum[:, :, None, :]
    weights = jnp.exp(jnp.where(inside[:, None], gap, -1e30))
    intersection = jnp.einsum("cin,cjn->cij", c_blocks, b_blocks, precision=PRECISE)
    weights = weights * intersection[:, None]
    within = jnp.einsum("chij,chjp->chip", weights, x_blocks, precision=PRECISE)
    last_seg = seg_blocks[:, -1]
    final = decay_sum[:, :, -1]
    tail = (seg_blocks == last_seg[:, None]).astype(jnp.float32)[:, None, :] * jnp.exp(
        final[:, :, None] - decay_sum
    )
    block_state = jnp.einsum(
        "chjp,cjn->chpn", x_blocks * tail[..., None], b_blocks, precision=PRECISE
    )
    carry_on = (last_seg[1:] == last_seg[:-1]).astype(jnp.float32)
    factor = jnp.exp(final[1:]) * carry_on[:, None]
    state = jnp.zeros((heads, head_dim, nstate), jnp.float32)
    entering = [state]
    for number in range(count - 1):
        if number == 0:
            state = block_state[0]
        else:
            state = factor[number - 1][:, None, None] * state + block_state[number]
        entering.append(state)
    entering = jnp.stack(entering)
    previous = jnp.concatenate([jnp.full((1,), -3, jnp.int32), last_seg[:-1]])
    head_weight = (seg_blocks == previous[:, None]).astype(jnp.float32)[:, None, :] * jnp.exp(
        decay_sum
    )
    carried = (
        jnp.einsum("cin,chpn->chip", c_blocks, entering, precision=PRECISE)
        * head_weight[..., None]
    )
    return (within + carried).transpose(0, 2, 1, 3).reshape(total, heads, head_dim)


def mixer_core(gate_and_x, step_raw, state_maps, conv_x, conv_bc, head_params, segments):
    total = gate_and_x.shape[0]
    heads = step_raw.shape[1]
    z_part = gate_and_x[:, 0]
    x_part = jax.nn.silu(causal_filter(gate_and_x[:, 1], conv_x, segments))
    maps = jax.nn.silu(causal_filter(state_maps, conv_bc, segments))
    nstate = state_maps.shape[1] // 2
    x_heads = x_part.reshape(total, heads, SSM_HEAD_DIM)
    rates = jnp.exp(head_params[0])
    steps = jax.nn.softplus(step_raw + head_params[1][None, :])
    output = state_space(x_heads, steps, rates, maps[:, :nstate], maps[:, nstate:], segments)
    output = output + head_params[2][None, :, None] * x_heads
    return output.reshape(total, heads * SSM_HEAD_DIM) * jax.nn.silu(z_part)


def block_scores(queries, keys, segments, start, stop, scale):
    part = queries[start:stop]
    scores = jnp.einsum(
        "ikgd,jkd->kgij", part, keys[:stop], preferred_element_type=jnp.float32
    ) * scale
    rows_here = jnp.arange(start, stop, dtype=jnp.int32)
    index = jnp.arange(stop, dtype=jnp.int32)
    allowed = (segments[start:stop, None] == segments[None, :stop]) & (
        rows_here[:, None] >= index[None, :]
    )
    return jnp.where(allowed[None, None], scores, -1e30)


def attend(queries, keys, values, segments):
    total = queries.shape[0]
    block = min(ATT_BLOCK, total)
    scale = queries.shape[-1] ** (-0.5)
    outputs, log_sums = [], []
    for start in range(0, total, block):
        stop = start + block
        scores = block_scores(queries, keys, segments, start, stop, scale)
        log_sum = jax.nn.logsumexp(scores, axis=-1)
        probs = jnp.exp(scores - log_sum[..., None]).astype(jnp.bfloat16)
        outputs.append(
            jnp.einsum("kgij,jkd->ikgd", probs, values[:stop], preferred_element_type=jnp.float32)
        )
        log_sums.append(log_sum)
    return (jnp.concatenate(outputs), log_sums)


def attend_back(queries, keys, values, segments, log_sums, grad_out):
    total = queries.shape[0]
    block = min(ATT_BLOCK, total)
    scale = queries.shape[-1] ** (-0.5)
    grad_parts = []
    grad_keys = jnp.zeros(keys.shape, jnp.float32)
    grad_values = jnp.zeros(keys.shape, jnp.float32)
    for number, start in enumerate(range(0, total, block)):
        stop = start + block
        part = queries[start:stop]
        part_grad = grad_out[start:stop]
        scores = block_scores(queries, keys, segments, start, stop, scale)
        probs = jnp.exp(scores - log_sums[number][..., None])
        grad_probs = jnp.einsum(
            "ikgd,jkd->kgij", part_grad, values[:stop], preferred_element_type=jnp.float32
        )
        grad_scores = (
            probs * (grad_probs - jnp.sum(probs * grad_probs, axis=-1, keepdims=True))
        ).astype(jnp.bfloat16)
        grad_parts.append(
            jnp.einsum(
                "kgij,jkd->ikgd", grad_scores, keys[:stop], preferred_element_type=jnp.float32
            )
            * scale
        )
        key_part = (
            jnp.einsum("kgij,ikgd->jkd", grad_scores, part, preferred_element_type=jnp.float32)
            * scale
        )
        value_part = jnp.einsum(
            "kgij,ikgd->jkd",
            probs.astype(jnp.bfloat16),
            part_grad,
            preferred_element_type=jnp.float32,
        )
        grad_keys = grad_keys.at[:stop].add(key_part)
        grad_values = grad_values.at[:stop].add(value_part)
    return (jnp.concatenate(grad_parts), grad_keys, grad_values)


def other_half(values):
    halves = lax.axis_size("tensor")
    return lax.ppermute(values, "tensor", [(i, (i + 1) % halves) for i in range(halves)])


def on_device(
    tokens,
    out_grad,
    segment_ids,
    norm_gains,
    w_zx,
    w_bc,
    w_dt,
    conv_x,
    conv_bc,
    head_params,
    ssm_gain,
    w_out,
    w_q,
    w_kv,
    w_o,
    w_gate_up,
    w_down,
):
    total, width = tokens.shape
    inner_local = w_zx.shape[2]
    heads_local = w_dt.shape[1]
    hidden_local = w_gate_up.shape[2]
    nmaps = w_bc.shape[1]
    key_heads = w_kv.shape[2] // ATT_HEAD_DIM
    query_heads = w_q.shape[1] // ATT_HEAD_DIM
    group = query_heads // key_heads
    key_width = key_heads * ATT_HEAD_DIM
    query_width = query_heads * ATT_HEAD_DIM
    gate_up_weight = w_gate_up.reshape(width, 2 * hidden_local)
    step_pad = -heads_local % 128
    in_weight = jnp.concatenate(
        [
            w_zx.reshape(width, 2 * inner_local),
            w_q,
            w_kv.reshape(width, 2 * key_width),
            w_bc,
            jnp.pad(w_dt, ((0, 0), (0, step_pad))),
        ],
        axis=1,
    )
    at_q = 2 * inner_local
    at_kv = at_q + query_width
    at_bc = at_kv + 2 * key_width
    at_dt = at_bc + nmaps
    resid = tokens.astype(jnp.float32)
    live = (segment_ids >= 0).astype(jnp.float32)[:, None]
    cotangent = (out_grad.astype(jnp.float32) * live).astype(jnp.bfloat16)
    scale_in = norm_scale(resid)
    unit_in = resid * scale_in
    normed_in = (unit_in * norm_gains[0][None, :]).astype(jnp.bfloat16)
    projected = product(normed_in, in_weight)
    gate_and_x = projected[:, :at_q].reshape(total, 2, inner_local)
    state_maps = projected[:, at_bc:at_dt]
    step_raw = projected[:, at_dt : at_dt + heads_local]

    def local_mixer(first, second, third, fourth, fifth, sixth):
        return mixer_core(first, second, third, fourth, fifth, sixth, segment_ids)

    gated, mixer_pullback = jax.vjp(
        local_mixer, gate_and_x, step_raw, state_maps, conv_x, conv_bc, head_params
    )
    squares = lax.psum(jnp.sum(gated * gated, axis=1), "tensor")
    scale_ssm = lax.rsqrt(squares[:, None] / INNER + EPS)
    unit_ssm = gated * scale_ssm
    mixed_ssm = (unit_ssm * ssm_gain[None, :]).astype(jnp.bfloat16)
    cosines, sines = rotary_tables(token_places(segment_ids), ATT_HEAD_DIM)
    queries = projected[:, at_q:at_kv].reshape(total, query_heads, ATT_HEAD_DIM)
    key_vals = projected[:, at_kv:at_bc].reshape(total, 2, key_heads, ATT_HEAD_DIM)
    queries = (
        rotate(queries, cosines, sines)
        .astype(jnp.bfloat16)
        .reshape(total, key_heads, group, ATT_HEAD_DIM)
    )
    keys = rotate(key_vals[:, 0], cosines, sines).astype(jnp.bfloat16)
    values = key_vals[:, 1].astype(jnp.bfloat16)
    attended, log_sums = attend(queries, keys, values, segment_ids)
    attended = attended.astype(jnp.bfloat16).reshape(total, query_width)
    mixed_in = jnp.concatenate([mixed_ssm, attended], axis=1)
    mix_weight = jnp.concatenate([w_out, w_o], axis=0)
    piece = total // PIECES
    middle, middle_down, unit_mid, scale_mid = [], [], [], []
    normed_mid, activation, delta_gate_up, delta_partial = [], [], [], []
    mix_parts = [
        product(mixed_in[n * piece : (n + 1) * piece], mix_weight) for n in range(PIECES)
    ]
    mix_sent = [other_half(part) for part in mix_parts]
    for n in range(PIECES):
        rows = slice(n * piece, (n + 1) * piece)
        middle_n = resid[rows] + (mix_parts[n] + mix_sent[n])
        scale_n = norm_scale(middle_n)
        unit_n = middle_n * scale_n
        normed_n = (unit_n * norm_gains[1][None, :]).astype(jnp.bfloat16)
        gate_up = product(normed_n, gate_up_weight)
        gate = gate_up[:, :hidden_local]
        upper = gate_up[:, hidden_local:]
        delta_act = product_back(cotangent[rows], w_down)
        sigma = jax.nn.sigmoid(gate)
        activation_n = (gate * sigma * upper).astype(jnp.bfloat16)
        delta_gate = delta_act * upper * sigma * (1.0 + gate * (1.0 - sigma))
        delta_upper = delta_act * (gate * sigma)
        delta_n = jnp.concatenate([delta_gate, delta_upper], axis=1).astype(jnp.bfloat16)
        partial_n = product_back(delta_n, gate_up_weight)
        middle.append(middle_n)
        scale_mid.append(scale_n)
        unit_mid.append(unit_n)
        normed_mid.append(normed_n)
        activation.append(activation_n)
        delta_gate_up.append(delta_n)
        delta_partial.append(partial_n)
    delta_sent = [other_half(part) for part in delta_partial]
    activation = jnp.concatenate(activation)
    delta_gate_up = jnp.concatenate(delta_gate_up)
    normed_mid = jnp.concatenate(normed_mid)
    feed_grads = jnp.concatenate(
        [weight_product(normed_mid, delta_gate_up), weight_product(cotangent, activation)], axis=1
    )
    gain_mid = sum(jnp.sum(part * unit, axis=0) for part, unit in zip(delta_partial, unit_mid))
    delta_middle = jnp.concatenate(
        [
            norm_back(part + sent, unit, scale, norm_gains[1])
            for part, sent, unit, scale in zip(delta_partial, delta_sent, unit_mid, scale_mid)
        ]
    ) + cotangent.astype(jnp.float32)
    delta_middle, feed_grads = lax.optimization_barrier((delta_middle, feed_grads))
    feed_grads = lax.psum_scatter(feed_grads, "dp", scatter_dimension=0, tiled=True)
    delta_mix = delta_middle.astype(jnp.bfloat16)
    out_part = product(activation, w_down)
    out_sent = other_half(out_part)
    mix_grads = weight_product(delta_mix, mixed_in)
    delta_ssm = product_back(delta_mix, w_out)
    delta_attended = (
        product_back(delta_mix, w_o)
        .astype(jnp.bfloat16)
        .reshape(total, key_heads, group, ATT_HEAD_DIM)
    )
    grad_ssm_gain = jnp.sum(delta_ssm * unit_ssm, axis=0)
    delta_unit = delta_ssm * ssm_gain[None, :]
    across = lax.psum(jnp.sum(delta_unit * gated, axis=1), "tensor")
    delta_gated = scale_ssm * delta_unit - gated * scale_ssm**3 * (across[:, None] / INNER)
    delta_gx, delta_step, delta_maps, grad_conv_x, grad_conv_bc, grad_heads = mixer_pullback(
        delta_gated
    )
    delta_queries, delta_keys, delta_values = attend_back(
        queries, keys, values, segment_ids, log_sums, delta_attended
    )
    delta_queries = rotate_back(
        delta_queries.reshape(total, query_heads, ATT_HEAD_DIM), cosines, sines
    ).reshape(total, query_width)
    delta_keys = rotate_back(delta_keys, cosines, sines).reshape(total, key_width)
    delta_in = jnp.concatenate(
        [
            delta_gx.reshape(total, 2 * inner_local).astype(jnp.bfloat16),
            delta_queries.astype(jnp.bfloat16),
            delta_keys.astype(jnp.bfloat16),
            delta_values.reshape(total, key_width).astype(jnp.bfloat16),
            delta_maps.astype(jnp.bfloat16),
            jnp.pad(delta_step, ((0, 0), (0, step_pad))).astype(jnp.bfloat16),
        ],
        axis=1,
    )
    in_part = product_back(delta_in, in_weight)
    in_sent = other_half(in_part)
    in_grads = weight_product(normed_in, delta_in)
    mix_grads, feed_grads = lax.optimization_barrier((mix_grads, feed_grads))
    mix_grads = lax.psum_scatter(mix_grads, "dp", scatter_dimension=0, tiled=True)
    in_grads, mix_grads = lax.optimization_barrier((in_grads, mix_grads))
    in_grads = lax.psum_scatter(in_grads, "dp", scatter_dimension=0, tiled=True)
    gain_in = jnp.sum(in_part * unit_in, axis=0)
    inner_n = conv_x.shape[0] * inner_local
    maps_n = conv_bc.shape[0] * nmaps
    small = jnp.concatenate(
        [
            grad_conv_bc.reshape(maps_n),
            gain_in,
            gain_mid,
            grad_conv_x.reshape(inner_n),
            grad_ssm_gain,
            grad_heads.reshape(-1),
        ]
    )
    small = lax.psum(small, "dp")
    at_conv = maps_n + 2 * width
    at_gain = at_conv + inner_n
    at_heads = at_gain + inner_local
    grad_conv_x = small[at_conv:at_gain].reshape(conv_x.shape)
    grad_ssm_gain = small[at_gain:at_heads]
    grad_heads = small[at_heads:].reshape(head_params.shape)
    halves = lax.axis_size("tensor")
    where_tensor = lax.axis_index("tensor")
    bc_rows = in_grads[:, at_bc:at_dt]
    shared, bc_rows = lax.psum((small[:at_conv], bc_rows), "tensor")
    bc_size = bc_rows.shape[0] // halves
    grad_bc = lax.dynamic_slice_in_dim(bc_rows, where_tensor * bc_size, bc_size, 0)
    place = lax.axis_index("dp") * halves + where_tensor
    count = lax.axis_size("dp") * halves
    conv_cols = nmaps // count
    gain_cols = width // count
    grad_conv_bc = lax.dynamic_slice_in_dim(
        shared[:maps_n].reshape(conv_bc.shape), place * conv_cols, conv_cols, 1
    )
    grad_gains = lax.dynamic_slice_in_dim(
        shared[maps_n:].reshape(2, width), place * gain_cols, gain_cols, 1
    )
    grad_tokens = (
        norm_back(in_part + in_sent, unit_in, scale_in, norm_gains[0]) + delta_middle
    )
    mixed = (jnp.concatenate(middle) + (out_part + out_sent)).astype(jnp.bfloat16)
    mine = in_grads.shape[0]
    grad_zx = in_grads[:, :at_q].reshape(mine, 2, inner_local)
    grad_q = in_grads[:, at_q:at_kv]
    grad_kv = in_grads[:, at_kv:at_bc].reshape(mine, 2, key_width)
    grad_dt = in_grads[:, at_dt : at_dt + heads_local]
    grad_gate_up = feed_grads[:, : 2 * hidden_local].reshape(mine, 2, hidden_local)
    grad_down = feed_grads[:, 2 * hidden_local :].T
    grad_out = mix_grads[:, :inner_local].T
    grad_o = mix_grads[:, inner_local:].T
    return (
        mixed,
        grad_tokens,
        grad_gains,
        grad_zx,
        grad_bc,
        grad_dt,
        grad_conv_x,
        grad_conv_bc,
        grad_heads,
        grad_ssm_gain,
        grad_out,
        grad_q,
        grad_kv,
        grad_o,
        grad_gate_up,
        grad_down,
    )


def solution(mesh):
    return jax.shard_map(
        on_device,
        mesh=mesh,
        in_specs=(
            P("dp", None),
            P("dp", None),
            P("dp"),
            P(),
            P(None, None, "tensor"),
            P(),
            P(None, "tensor"),
            P(None, "tensor"),
            P(),
            P(None, "tensor"),
            P("tensor"),
            P("tensor", None),
            P(None, "tensor"),
            P(None, None, "tensor"),
            P("tensor", None),
            P(None, None, "tensor"),
            P("tensor", None),
        ),
        out_specs=(
            P("dp", None),
            P("dp", None),
            P(None, ("dp", "tensor")),
            P("dp", None, "tensor"),
            P(("dp", "tensor"), None),
            P("dp", "tensor"),
            P(None, "tensor"),
            P(None, ("dp", "tensor")),
            P(None, "tensor"),
            P("tensor"),
            P("tensor", "dp"),
            P("dp", "tensor"),
            P("dp", None, "tensor"),
            P("tensor", "dp"),
            P("dp", None, "tensor"),
            P("tensor", "dp"),
        ),
        check_vma=False,
    )
```
